256 devices in a mesh: gx: 8 (over z), gy: 8 (over x_hi, y), gz: 4 (over x_lo, core).
Axes of the slice: x: 4 (x_hi: 2, x_lo: 2; x = x_hi * 2 + x_lo), y: 4, z: 8, core: 2. Of those that a mesh axis runs over, the one named last changes fastest.
Arguments:
- tokens: bfloat16 [1536, 6144], P('gz', 'gy'), may hold values from -6 to 6
- up_weight: bfloat16 [6144, 24576], P(('gy', 'gz'), 'gx'), may hold values from -0.078125 to 0.078125
- down_weight: bfloat16 [24576, 6144], P(('gx', 'gz'), 'gy'), may hold values from -0.0390625 to 0.0390625
- upstream: bfloat16 [1536, 6144], P('gz', 'gy'), may hold values from -1.1953125 to 1.1953125
Outputs:
- mlp_output: bfloat16 [1536, 6144], P('gz', ('gy', 'gx'))
- token_grad: bfloat16 [1536, 6144], P('gz', ('gy', 'gx'))
- up_grad: bfloat16 [6144, 24576], P(('gy', 'gz'), 'gx')
- down_grad: bfloat16 [24576, 6144], P(('gx', 'gz'), 'gy')
The draws below stay inside these ranges and needn't reach their ends.
All inputs are finite; a program needn't handle non-finite values.
Results may differ from the reference program's by a relative error of at most 0.028.
Values may be sent and summed in bfloat16 or wider, within the bound.
No kernel may reach another device: no remote copies, remote signals or barrier semaphores. Data moves between devices by JAX's collectives and lax.ppermute only.
A program may use at most 128 MiB of HBM per device.

```python
import jax
import jax.numpy as jnp
from jax import lax

D = 6144
FF = 24576
TOK_DEV = 384
TOKENS = 1536


def raised(values, key, source, target, shards_of, factor):
    owner, partner = [(jnp.arange(values.shape[dim]) // (values.shape[dim] // shards_of)).reshape([-1 if axis == dim else 1 for axis in range(values.ndim)]) for dim in (source, target)]
    chosen = jax.random.permutation(key, shards_of)[partner]
    strong = (owner == chosen) | (owner == (partner + shards_of // 2) % shards_of)
    return jnp.where(strong, factor * values, values)


def block_levels(key, shape, pieces, low, largest):
    def one(dim, blocks):
        draws = jax.random.uniform(jax.random.fold_in(jax.random.fold_in(key, 6), dim), (blocks,), jnp.float32, low / len(pieces), largest / len(pieces))
        return jnp.repeat(jnp.exp(draws), shape[dim] // blocks).reshape((-1,) + (1,) * (len(shape) - dim - 1))

    gain = one(*pieces[0])
    for cut in pieces[1:]:
        gain = gain * one(*cut)
    return gain


def normal_values(own_key, shape, spread, limit, pieces=(), held_as=jnp.bfloat16):
    result = spread * jax.random.normal(own_key, shape, jnp.float32)
    if pieces:
        result = result * block_levels(own_key, shape, pieces, -0.22, 0.18)
    return jnp.clip(result, -limit, limit).astype(held_as)


def noise_with(own_key, shape, width, bound, shards, heavy, kind=jnp.bfloat16):
    entries = width * jax.random.normal(own_key, shape, jnp.float32)
    if shards:
        entries = entries * block_levels(own_key, shape, shards, -0.22, 0.18)
    return jnp.clip(raised(entries, jax.random.fold_in(own_key, 3), *heavy), -bound, bound).astype(kind)


def setup_inputs(seed: int = 0) -> dict:
    splits = jax.random.split(jax.random.key(seed), 5)
    tokens = noise_with(splits[0], (TOKENS, D), 1.0, 6.0, ((0, 4), (1, 8)), (0, 1, 8, 2.0))
    up_weight = normal_values(splits[1], (D, FF), D ** -0.5, 0.078125, ((0, 32), (1, 8)))
    down_weight = normal_values(splits[2], (FF, D), FF ** -0.5, 0.0390625, ((0, 32), (1, 8)))
    upstream = normal_values(splits[3], (TOKENS, D), 0.2, 1.1953125, ((0, 4), (1, 8)))
    return {"tokens": tokens, "up_weight": up_weight, "down_weight": down_weight, "upstream": upstream}


coeff = 0.7978845608028654
cubic = 0.044715


def gelu_value(hidden):
    inner = jnp.tanh(coeff * (hidden + cubic * hidden * hidden * hidden))
    return 0.5 * hidden * (1.0 + inner)


def gelu_slope(hidden):
    inner = jnp.tanh(coeff * (hidden + cubic * hidden * hidden * hidden))
    return 0.5 * (1.0 + inner) + 0.5 * hidden * (1.0 - inner * inner) * coeff * (1.0 + 3.0 * cubic * hidden * hidden)


def rounded(value):
    return lax.optimization_barrier(value.astype(jnp.bfloat16)).astype(jnp.float32)


def reference(tokens, up_weight, down_weight, upstream):
    pre = jnp.dot(tokens, up_weight, preferred_element_type=jnp.float32)
    act = gelu_value(pre).astype(jnp.bfloat16)
    mlp_output = jnp.dot(act, down_weight, preferred_element_type=jnp.float32).astype(jnp.bfloat16)
    act_grad = jnp.dot(upstream, down_weight.T, preferred_element_type=jnp.float32)
    pre_grad = (act_grad * gelu_slope(pre)).astype(jnp.bfloat16)
    token_grad = jnp.dot(pre_grad, up_weight.T, preferred_element_type=jnp.float32).astype(jnp.bfloat16)

    def accumulate(carry, index):
        start = (index * TOK_DEV).astype(jnp.int32)
        token_block = lax.dynamic_slice_in_dim(tokens, start, TOK_DEV, 0)
        grad_block = lax.dynamic_slice_in_dim(pre_grad, start, TOK_DEV, 0)
        act_block = lax.dynamic_slice_in_dim(act, start, TOK_DEV, 0)
        up_block = lax.dynamic_slice_in_dim(upstream, start, TOK_DEV, 0)
        up_term = rounded(jnp.dot(token_block.T, grad_block, preferred_element_type=jnp.float32))
        down_term = rounded(jnp.dot(act_block.T, up_block, preferred_element_type=jnp.float32))
        return (carry[0] + up_term, carry[1] + down_term), None

    start_sums = (jnp.zeros((D, FF), jnp.float32), jnp.zeros((FF, D), jnp.float32))
    sums, _ = lax.scan(accumulate, start_sums, jnp.arange(TOKENS // TOK_DEV, dtype=jnp.int32))
    up_grad = sums[0].astype(jnp.bfloat16)
    down_grad = sums[1].astype(jnp.bfloat16)
    return mlp_output, token_grad, up_grad, down_grad
```

```python
import jax
import jax.numpy as jnp
from jax import lax
from jax.sharding import PartitionSpec as P

coeff = 0.7978845608028654
cubic = 0.044715
f32 = jnp.float32
bf16 = jnp.bfloat16


def gelu_both(hidden):
    square = hidden * hidden
    inner = jnp.tanh(coeff * (hidden + cubic * hidden * square))
    value = 0.5 * hidden * (1.0 + inner)
    slope = 0.5 * (1.0 + inner) + 0.5 * hidden * (1.0 - inner * inner) * coeff * (
        1.0 + 3.0 * cubic * square
    )
    return value, slope


def to_group(x, flip):
    return lax.ppermute(x, "gz", [(i, i ^ flip) for i in range(4)])


def to_row(x, shift):
    return lax.ppermute(x, "gy", [(i, (i // 4) * 4 + (i + shift) % 4) for i in range(8)])


def to_half(x):
    return lax.ppermute(x, "gy", [(i, i ^ 4) for i in range(8)])


def gather_tokens(own):
    core = to_group(own, 1)
    far = to_group(own, 2)
    diagonal = to_group(far, 1)
    return (own, core), (far, diagonal)


def spread_weight(shard, place):
    full = jnp.zeros((768, 768), bf16)
    for flip in (2, 3, 1, 0):
        other = place ^ flip
        piece = lax.dynamic_slice_in_dim(shard, other * 768, 768, 1)
        if flip:
            piece = to_group(piece, flip)
        full = lax.dynamic_update_slice_in_dim(full, piece, other * 192, 0)
    return full


def collect_weight(full, place):
    shard = jnp.zeros((192, 3072), bf16)
    for flip in (2, 3, 1, 0):
        other = place ^ flip
        piece = lax.dynamic_slice_in_dim(full, other * 192, 192, 0)
        if flip:
            piece = to_group(piece, flip)
        shard = lax.dynamic_update_slice_in_dim(shard, piece, other * 768, 1)
    return shard


def sum_rows(parts, high):
    cut = jnp.stack([p.reshape(4, 2, 48, 768) for p in parts], 1)
    total = cut[0].astype(f32)
    for shift in (1, 3, 2):
        total = total + to_row(cut[shift], shift).astype(f32)
    mine = jnp.where(high, total[:, 1], total[:, 0])
    theirs = jnp.where(high, total[:, 0], total[:, 1]).astype(bf16)
    return mine + to_half(theirs).astype(f32)


def gather_rows(own, high):
    other = to_half(own)
    pair = jnp.where(high, jnp.stack([other, own], 1), jnp.stack([own, other], 1))
    up, down, across = to_row(pair, 1), to_row(pair, 3), to_row(pair, 2)
    return [
        jnp.concatenate([pair[r], down[r], across[r], up[r]], 0).reshape(384, 768)
        for r in range(2)
    ]


def product(a, b, da, db):
    return lax.dot_general(a, b, (((da,), (db,)), ((), ())), preferred_element_type=f32)


def sum_cores(weight, blocks, contract):
    keep = product(weight, blocks[0], contract, 1)
    send = product(weight, blocks[1], contract, 1).astype(bf16)
    return keep + to_group(send, 1).astype(f32)


def finish(near, far, shift):
    total = (near + to_group(far.astype(bf16), 2).astype(f32)).astype(bf16)
    got = lax.all_to_all(total.reshape(8, 96, 384), "gx", 0, 0, tiled=True)
    out = jnp.sum(got.astype(f32), 0).astype(bf16).T.reshape(4, 96, 96)
    return jnp.roll(out, shift, 0).reshape(384, 96)


def body(tokens, up_weight, down_weight, upstream):
    gy = lax.axis_index("gy")
    gz = lax.axis_index("gz")
    row = gy % 4
    high = gy >= 4

    tokens = jnp.roll(tokens.reshape(4, 96, 768), -row, 0).reshape(384, 768)
    upstream = jnp.roll(upstream.reshape(4, 96, 768), -row, 0).reshape(384, 768)

    ups = gather_tokens(upstream)
    up_full = spread_weight(up_weight, gz)
    toks = gather_tokens(tokens)

    act_grad = [
        sum_rows([product(u, down_weight, 1, 1).astype(bf16) for u in pair], high) for pair in ups
    ]
    pre = [sum_rows([product(t, up_full, 1, 0).astype(bf16) for t in pair], high) for pair in toks]
    act, pre_grad = [], []
    for c in range(2):
        value, slope = gelu_both(pre[c])
        act.append(value.astype(bf16))
        pre_grad.append((act_grad[c] * slope).astype(bf16))

    grads = [gather_rows(p, high) for p in pre_grad]
    token_parts = []
    for c in range(2):
        token_parts.append(sum_cores(up_full, grads[c], 1))
    token_grad = finish(token_parts[0], token_parts[1], row)
    all_grads = jnp.concatenate(grads[0] + grads[1], 0)
    all_tokens = jnp.concatenate(list(toks[0] + toks[1]), 0)
    up_grad = collect_weight(product(all_tokens, all_grads, 0, 0).astype(bf16), gz)

    acts = [gather_rows(a, high) for a in act]
    out_parts = [sum_cores(down_weight, acts[c], 0) for c in range(2)]
    mlp_output = finish(out_parts[0], out_parts[1], row)
    all_acts = jnp.concatenate(acts[0] + acts[1], 0)
    all_ups = jnp.concatenate(list(ups[0] + ups[1]), 0)
    down_grad = product(all_acts, all_ups, 0, 0).astype(bf16)
    return (mlp_output, token_grad, up_grad, down_grad)


def solution(mesh):
    return jax.shard_map(
        body,
        mesh=mesh,
        in_specs=(P("gz", "gy"), P(("gy", "gz"), "gx"), P(("gx", "gz"), "gy"), P("gz", "gy")),
        out_specs=(
            P("gz", ("gy", "gx")),
            P("gz", ("gy", "gx")),
            P(("gy", "gz"), "gx"),
            P(("gx", "gz"), "gy"),
        ),
        check_vma=False,
    )
```

```python
import jax
import jax.numpy as jnp
from jax import lax
from jax.sharding import PartitionSpec as P

coeff = 0.7978845608028654
cubic = 0.044715
f32 = jnp.float32
bf16 = jnp.bfloat16


def gelu_both(hidden):
    square = hidden * hidden
    inner = jnp.tanh(coeff * (hidden + cubic * hidden * square))
    value = 0.5 * hidden * (1.0 + inner)
    slope = 0.5 * (1.0 + inner) + 0.5 * hidden * (1.0 - inner * inner) * coeff * (
        1.0 + 3.0 * cubic * square
    )
    return value, slope


def to_group(x, flip):
    return lax.ppermute(x, "gz", [(i, i ^ flip) for i in range(4)])


def to_row(x, shift):
    return lax.ppermute(x, "gy", [(i, (i // 4) * 4 + (i + shift) % 4) for i in range(8)])


def to_half(x):
    return lax.ppermute(x, "gy", [(i, i ^ 4) for i in range(8)])


def after(x, *needed):
    return lax.optimization_barrier((x,) + needed)[0]


def spread_weight(shard, chip):
    send = lax.dynamic_slice_in_dim(shard, (1 - chip) * 1536, 1536, 1)
    return lax.dynamic_slice_in_dim(shard, chip * 1536, 1536, 1), to_group(send, 2)


def spread_cores(own, far, chip, core):
    both = jnp.stack([jnp.where(chip == 0, own, far), jnp.where(chip == 0, far, own)])
    mine = jnp.where(core == 0, both[:, :, :768], both[:, :, 768:])
    theirs = jnp.where(core == 0, both[:, :, 768:], both[:, :, :768])
    got = to_group(theirs, 1)
    return jnp.where(
        core == 0, jnp.stack([mine, got], 1), jnp.stack([got, mine], 1)
    ).reshape(768, 768)


def collect_far(full, chip):
    halves = full.reshape(2, 2, 192, 768)
    send = jnp.where(chip == 0, halves[1], halves[0])
    return jnp.where(chip == 0, halves[0], halves[1]), to_group(send, 2)


def collect_cores(own, far, chip, core):
    both = jnp.stack([jnp.where(chip == 0, own, far), jnp.where(chip == 0, far, own)])
    mine = jnp.where(core == 0, both[:, 0], both[:, 1])
    theirs = jnp.where(core == 0, both[:, 1], both[:, 0])
    got = to_group(theirs, 1)
    first = jnp.where(core == 0, mine, got)
    second = jnp.where(core == 0, got, mine)
    return jnp.concatenate([first[0], second[0], first[1], second[1]], 1)


def send_rows(parts):
    cut = jnp.stack([p.reshape(4, 2, 48, 768) for p in parts], 1)
    return [cut[0]] + [to_row(cut[shift], shift) for shift in (1, 3, 2)]


def send_half(got, high):
    total = sum(g.astype(f32) for g in got)
    mine = jnp.where(high, total[:, 1], total[:, 0])
    theirs = jnp.where(high, total[:, 0], total[:, 1]).astype(bf16)
    return mine, to_half(theirs)


def pair_half(own, high):
    other = to_half(own)
    return jnp.where(high, jnp.stack([other, own], 1), jnp.stack([own, other], 1))


def gather_rows(pair):
    return pair, to_row(pair, 1), to_row(pair, 3), to_row(pair, 2)


def blocks_of(got):
    pair, up, down, across = got
    return [
        jnp.concatenate([pair[r], down[r], across[r], up[r]], 0).reshape(384, 768)
        for r in range(2)
    ]


def product(a, b, da, db):
    return lax.dot_general(a, b, (((da,), (db,)), ((), ())), preferred_element_type=f32)


def sum_cores(weight, blocks, contract):
    send = product(weight, blocks[1], contract, 1).astype(bf16)
    got = to_group(send, 1)
    return product(weight, blocks[0], contract, 1) + got.astype(f32)


def over_columns(near, far):
    total = (near + far.astype(f32)).astype(bf16)
    return lax.all_to_all(total.reshape(8, 96, 384), "gx", 0, 0, tiled=True)


def finish(got, shift):
    out = jnp.sum(got.astype(f32), 0).astype(bf16).T.reshape(4, 96, 96)
    return jnp.roll(out, shift, 0).reshape(384, 96)


def body(tokens, up_weight, down_weight, upstream):
    gy = lax.axis_index("gy")
    gz = lax.axis_index("gz")
    row = gy % 4
    high = gy >= 4
    chip, core = gz // 2, gz % 2

    ups = jnp.roll(upstream.reshape(4, 96, 768), -row, 0).reshape(384, 768)
    ups_far = to_group(ups, 2)
    ups_core = to_group(ups, 1)
    up_own, up_far = spread_weight(after(up_weight, ups), chip)
    shares = [product(u, down_weight, 1, 1).astype(bf16) for u in (ups, ups_core)]
    grad_near = send_rows(shares)

    ups_far = after(ups_far, *shares)
    ups_last = to_group(ups_far, 1)
    shares = [product(u, down_weight, 1, 1).astype(bf16) for u in (ups_far, ups_last)]
    shares = after(shares, grad_near[1], grad_near[2])
    grad_far = send_rows(shares)

    up_far = after(up_far, *shares)
    toks = jnp.roll(after(tokens, *shares).reshape(4, 96, 768), -row, 0).reshape(384, 768)
    toks_far = to_group(after(toks, up_far), 2)
    up_full = spread_cores(up_own, up_far, chip, core)
    toks_core = to_group(after(toks, up_full), 1)
    grad_mine, grad_theirs = send_half(grad_near, high)
    shares = [product(t, up_full, 1, 0).astype(bf16) for t in (toks, toks_core)]
    shares = after(shares, grad_far[1], grad_far[2])
    pre_near = send_rows(shares)

    grad_near = grad_mine + grad_theirs.astype(f32)
    toks_far, grad_near = after((toks_far, grad_near), *shares)
    toks_last = to_group(toks_far, 1)
    grad_mine, grad_theirs = send_half(grad_far, high)
    shares = [product(t, up_full, 1, 0).astype(bf16) for t in (toks_far, toks_last)]
    shares = after(shares, pre_near[1], pre_near[2])
    pre_far = send_rows(shares)
    grad_far = grad_mine + grad_theirs.astype(f32)

    pre_mine, pre_theirs = send_half(pre_near, high)
    pre_theirs, grad_far = after((pre_theirs, grad_far), *shares)
    value, slope = gelu_both(pre_mine + pre_theirs.astype(f32))
    act_near = value.astype(bf16)
    pre_grad_near = (grad_near * slope).astype(bf16)
    near_pair = pair_half(pre_grad_near, high)
    near_got = gather_rows(after(near_pair, pre_far[1], pre_far[2]))

    pre_mine, pre_theirs = send_half(pre_far, high)
    value, slope = gelu_both(pre_mine + pre_theirs.astype(f32))
    act_far = value.astype(bf16)
    pre_grad_far = (grad_far * slope).astype(bf16)
    far_pair = pair_half(pre_grad_far, high)
    far_got = gather_rows(after(far_pair, near_got[1], near_got[2]))

    act_far_pair = pair_half(after(act_far, far_pair), high)
    grads_near = blocks_of(near_got)
    token_near = sum_cores(up_full, grads_near, 1)
    act_far_pair, token_near = after((act_far_pair, token_near), far_got[1], far_got[2])
    act_far_got = gather_rows(act_far_pair)

    grads_far = blocks_of(far_got)
    token_far = to_group(sum_cores(up_full, grads_far, 1).astype(bf16), 2)
    all_grads = jnp.concatenate(grads_near + grads_far, 0)
    all_tokens = jnp.concatenate([toks, toks_core, toks_far, toks_last], 0)
    up_grad = product(all_tokens, all_grads, 0, 0).astype(bf16)
    act_near_pair = pair_half(after(act_near, far_got[1]), high)
    act_near_pair, up_grad = after((act_near_pair, up_grad), act_far_got[1], act_far_got[2])
    act_near_got = gather_rows(act_near_pair)

    token_got = over_columns(token_near, token_far)
    acts_far = blocks_of(act_far_got)
    out_far = to_group(sum_cores(down_weight, acts_far, 0).astype(bf16), 2)
    up_mine, up_theirs = collect_far(after(up_grad, token_far), chip)

    act_near_got = after(act_near_got, token_got)
    acts_near = blocks_of(act_near_got)
    out_near = sum_cores(down_weight, acts_near, 0)
    out_got = over_columns(out_near, out_far)

    up_out = collect_cores(up_mine, after(up_theirs, out_near), chip, core)
    token_grad = finish(after(token_got, out_near), row)
    mlp_output = finish(out_got, row)
    all_acts = jnp.concatenate(acts_near + acts_far, 0)
    all_ups = jnp.concatenate([ups, ups_core, ups_far, ups_last], 0)
    down_grad = product(all_acts, all_ups, 0, 0).astype(bf16)
    return (mlp_output, token_grad, up_out, down_grad)


def solution(mesh):
    return jax.shard_map(
        body,
        mesh=mesh,
        in_specs=(P("gz", "gy"), P(("gy", "gz"), "gx"), P(("gx", "gz"), "gy"), P("gz", "gy")),
        out_specs=(
            P("gz", ("gy", "gx")),
            P("gz", ("gy", "gx")),
            P(("gy", "gz"), "gx"),
            P(("gx", "gz"), "gy"),
        ),
        check_vma=False,
    )
```

```python
import jax
import jax.numpy as jnp
from jax import lax
from jax.sharding import PartitionSpec as P

coeff = 0.7978845608028654
cubic = 0.044715
f32 = jnp.float32
bf16 = jnp.bfloat16


def gelu_both(hidden):
    square = hidden * hidden
    inner = jnp.tanh(coeff * (hidden + cubic * hidden * square))
    value = 0.5 * hidden * (1.0 + inner)
    slope = 0.5 * (1.0 + inner) + 0.5 * hidden * (1.0 - inner * inner) * coeff * (
        1.0 + 3.0 * cubic * square
    )
    return value, slope


def to_group(x, flip):
    return lax.ppermute(x, "gz", [(i, i ^ flip) for i in range(4)])


def to_row(x, shift):
    return lax.ppermute(x, "gy", [(i, (i // 4) * 4 + (i + shift) % 4) for i in range(8)])


def to_half(x):
    return lax.ppermute(x, "gy", [(i, i ^ 4) for i in range(8)])


def after(x, *needed):
    return lax.optimization_barrier((x,) + needed)[0]


def spread_weight(shard, chip):
    send = lax.dynamic_slice_in_dim(shard, (1 - chip) * 1536, 1536, 1)
    return lax.dynamic_slice_in_dim(shard, chip * 1536, 1536, 1), to_group(send, 2)


def spread_cores(own, far, chip, core):
    both = jnp.stack([jnp.where(chip == 0, own, far), jnp.where(chip == 0, far, own)])
    mine = jnp.where(core == 0, both[:, :, :768], both[:, :, 768:])
    theirs = jnp.where(core == 0, both[:, :, 768:], both[:, :, :768])
    got = to_group(theirs, 1)
    return jnp.where(
        core == 0, jnp.stack([mine, got], 1), jnp.stack([got, mine], 1)
    ).reshape(768, 768)


def collect_far(full, chip):
    halves = full.reshape(2, 2, 192, 768)
    send = jnp.where(chip == 0, halves[1], halves[0])
    return jnp.where(chip == 0, halves[0], halves[1]), to_group(send, 2)


def collect_cores(own, far, chip, core):
    both = jnp.stack([jnp.where(chip == 0, own, far), jnp.where(chip == 0, far, own)])
    mine = jnp.where(core == 0, both[:, 0], both[:, 1])
    theirs = jnp.where(core == 0, both[:, 1], both[:, 0])
    got = to_group(theirs, 1)
    first = jnp.where(core == 0, mine, got)
    second = jnp.where(core == 0, got, mine)
    return jnp.concatenate([first[0], second[0], first[1], second[1]], 1)


def cut_rows(blocks, weight, contract):
    parts = [product(x, weight, 1, contract).astype(bf16) for x in blocks]
    return jnp.stack([p.reshape(4, 2, 48, 768) for p in parts], 1)


def send_rows(cut):
    return [cut[0]] + [to_row(cut[shift], shift) for shift in (1, 3, 2)]


def send_half(got, high):
    total = sum(g.astype(f32) for g in got)
    mine = jnp.where(high, total[:, 1], total[:, 0])
    theirs = jnp.where(high, total[:, 0], total[:, 1]).astype(bf16)
    return mine, to_half(theirs)


def pair_half(own, high):
    other = to_half(own)
    axis = own.ndim - 2
    return jnp.where(high, jnp.stack([other, own], axis), jnp.stack([own, other], axis))


def gather_rows(pair):
    return [pair, to_row(pair, 1), to_row(pair, 3), to_row(pair, 2)]


def blocks_of(got):
    pair, up, down, across = got
    return [
        jnp.concatenate([pair[r], down[r], across[r], up[r]], 0).reshape(384, 768)
        for r in range(2)
    ]


def product(a, b, da, db):
    return lax.dot_general(a, b, (((da,), (db,)), ((), ())), preferred_element_type=f32)


def sum_cores(weight, blocks, contract):
    send = product(weight, blocks[1], contract, 1).astype(bf16)
    got = to_group(send, 1)
    return product(weight, blocks[0], contract, 1) + got.astype(f32)


def finish(got, shift):
    out = jnp.sum(got.astype(f32), 0).astype(bf16).T.reshape(4, 96, 96)
    return jnp.roll(out, shift, 0).reshape(384, 96)


def body(tokens, up_weight, down_weight, upstream):
    gy = lax.axis_index("gy")
    gz = lax.axis_index("gz")
    row = gy % 4
    high = gy >= 4
    chip, core = gz // 2, gz % 2

    up_own, up_far = spread_weight(up_weight, chip)
    ups = jnp.roll(upstream.reshape(4, 96, 768), -row, 0).reshape(384, 768)
    ups_core = to_group(ups, 1)
    ups_far = to_group(after(ups, up_own), 2)
    cut = cut_rows((ups, ups_core), down_weight, 1)
    first = send_rows(cut)
    toks = jnp.roll(tokens.reshape(4, 96, 768), -row, 0).reshape(384, 768)
    toks_core = to_group(toks, 1)
    toks_far = to_group(after(toks, up_own), 2)

    up_full = spread_cores(up_own, after(up_far, cut), chip, core)
    cut = cut_rows((toks, toks_core), up_full, 0)
    first = after(first, cut)
    second = send_rows(after(cut, *first))
    grad_mine, grad_theirs = send_half(first, high)

    ups_last = to_group(ups_far, 1)
    cut = cut_rows((ups_far, ups_last), down_weight, 1)
    second = after(second, cut)
    third = send_rows(after(cut, *second))
    pre_mine, pre_theirs = send_half(second, high)

    toks_last = to_group(toks_far, 1)
    cut = cut_rows((toks_far, toks_last), up_full, 0)
    third = after(third, cut)
    fourth = send_rows(after(cut, *third))
    value, slope = gelu_both(pre_mine + pre_theirs.astype(f32))
    pre_grad = (grad_mine + grad_theirs.astype(f32)) * slope
    near = pair_half(jnp.stack([pre_grad, value]).astype(bf16), high)
    grad_near_pair, act_near_pair = near[0], near[1]
    grad_mine, grad_theirs = send_half(third, high)
    fourth = after(fourth, near)

    fifth = gather_rows(after(grad_near_pair, *fourth))
    pre_mine, pre_theirs = send_half(fourth, high)
    value, slope = gelu_both(pre_mine + pre_theirs.astype(f32))
    act_far = value.astype(bf16)
    pre_grad = ((grad_mine + grad_theirs.astype(f32)) * slope).astype(bf16)
    grad_far_pair = pair_half(pre_grad, high)
    fifth = after(fifth, grad_far_pair)
    sixth = gather_rows(after(grad_far_pair, *fifth))
    act_far_pair = pair_half(act_far, high)
    grads_near = blocks_of(fifth)
    token_near = sum_cores(up_full, grads_near, 1)
    sixth = after(sixth, act_far_pair)

    seventh = gather_rows(after(act_far_pair, *sixth))
    grads_far = blocks_of(sixth)
    token_far_sum = sum_cores(up_full, grads_far, 1).astype(bf16)
    token_far = to_group(token_far_sum, 2)
    all_grads = jnp.concatenate(grads_near + grads_far, 0)
    all_tokens = jnp.concatenate([toks, toks_core, toks_far, toks_last], 0)
    up_grad = product(all_tokens, all_grads, 0, 0).astype(bf16)
    seventh = after(seventh, token_far_sum, up_grad)
    up_mine, up_theirs = collect_far(after(up_grad, token_far_sum), chip)

    eighth = gather_rows(after(act_near_pair, *seventh))
    token_total = (token_near + token_far.astype(f32)).astype(bf16).reshape(8, 96, 384)
    token_got = lax.all_to_all(token_total, "gx", 0, 0, tiled=True)
    acts_far = blocks_of(after(seventh, token_total))
    out_far_sum = sum_cores(down_weight, acts_far, 0).astype(bf16)
    out_far = to_group(out_far_sum, 2)
    eighth = after(eighth, out_far_sum, up_theirs)

    acts_near = blocks_of(eighth)
    out_near = sum_cores(down_weight, acts_near, 0)
    out_total = (out_near + out_far.astype(f32)).astype(bf16).reshape(8, 96, 384)
    out_got = lax.all_to_all(after(out_total, token_got), "gx", 0, 0, tiled=True)

    up_out = collect_cores(up_mine, after(up_theirs, out_total), chip, core)
    token_grad = finish(after(token_got, out_total), row)
    mlp_output = finish(out_got, row)
    all_acts = jnp.concatenate(list(after(acts_near, out_total)) + acts_far, 0)
    all_ups = jnp.concatenate([ups, ups_core, ups_far, ups_last], 0)
    down_grad = product(all_acts, all_ups, 0, 0).astype(bf16)
    return (mlp_output, token_grad, up_out, down_grad)


def solution(mesh):
    return jax.shard_map(
        body,
        mesh=mesh,
        in_specs=(P("gz", "gy"), P(("gy", "gz"), "gx"), P(("gx", "gz"), "gy"), P("gz", "gy")),
        out_specs=(
            P("gz", ("gy", "gx")),
            P("gz", ("gy", "gx")),
            P(("gy", "gz"), "gx"),
            P(("gx", "gz"), "gy"),
        ),
        check_vma=False,
    )
```

```python
import jax
import jax.numpy as jnp
from jax import lax
from jax.sharding import PartitionSpec as P

coeff = 0.7978845608028654
cubic = 0.044715
f32 = jnp.float32
bf16 = jnp.bfloat16


def gelu_both(hidden):
    square = hidden * hidden
    inner = jnp.tanh(coeff * (hidden + cubic * hidden * square))
    value = 0.5 * hidden * (1.0 + inner)
    slope = 0.5 * (1.0 + inner) + 0.5 * hidden * (1.0 - inner * inner) * coeff * (
        1.0 + 3.0 * cubic * square
    )
    return value, slope


def to_group(x, flip):
    return lax.ppermute(x, "gz", [(i, i ^ flip) for i in range(4)])


def to_row(x, shift):
    return lax.ppermute(x, "gy", [(i, (i // 4) * 4 + (i + shift) % 4) for i in range(8)])


def to_half(x):
    return lax.ppermute(x, "gy", [(i, i ^ 4) for i in range(8)])


def after(x, *needed):
    return lax.optimization_barrier((x,) + needed)[0]


def spread_weight(shard, chip):
    send = lax.dynamic_slice_in_dim(shard, (1 - chip) * 1536, 1536, 1)
    return lax.dynamic_slice_in_dim(shard, chip * 1536, 1536, 1), to_group(send, 2)


def spread_cores(own, far, chip, core):
    both = jnp.stack([jnp.where(chip == 0, own, far), jnp.where(chip == 0, far, own)])
    mine = jnp.where(core == 0, both[:, :, :768], both[:, :, 768:])
    theirs = jnp.where(core == 0, both[:, :, 768:], both[:, :, :768])
    got = to_group(theirs, 1)
    return jnp.where(
        core == 0, jnp.stack([mine, got], 1), jnp.stack([got, mine], 1)
    ).reshape(768, 768)


def collect_far(full, chip):
    halves = full.reshape(2, 2, 192, 768)
    send = jnp.where(chip == 0, halves[1], halves[0])
    return jnp.where(chip == 0, halves[0], halves[1]), to_group(send, 2)


def collect_cores(own, far, chip, core):
    both = jnp.stack([jnp.where(chip == 0, own, far), jnp.where(chip == 0, far, own)])
    mine = jnp.where(core == 0, both[:, 0], both[:, 1])
    theirs = jnp.where(core == 0, both[:, 1], both[:, 0])
    got = to_group(theirs, 1)
    first = jnp.where(core == 0, mine, got)
    second = jnp.where(core == 0, got, mine)
    return jnp.concatenate([first[0], second[0], first[1], second[1]], 1)


def cut_rows(blocks, weight, contract):
    parts = [product(x, weight, 1, contract).astype(bf16) for x in blocks]
    return jnp.stack([p.reshape(4, 2, 48, 768) for p in parts], 1)


def send_rows(cut):
    return [cut[0]] + [to_row(cut[shift], shift) for shift in (1, 3, 2)]


def send_half(got, high):
    total = sum(g.astype(f32) for g in got)
    mine = jnp.where(high, total[:, 1], total[:, 0])
    theirs = jnp.where(high, total[:, 0], total[:, 1]).astype(bf16)
    return mine, to_half(theirs)


def pair_half(own, high):
    other = to_half(own)
    axis = own.ndim - 2
    return jnp.where(high, jnp.stack([other, own], axis), jnp.stack([own, other], axis))


def gather_rows(pair):
    return [pair, to_row(pair, 1), to_row(pair, 3), to_row(pair, 2)]


def blocks_of(got):
    pair, up, down, across = got
    return [
        jnp.concatenate([pair[r], down[r], across[r], up[r]], 0).reshape(384, 768)
        for r in range(2)
    ]


def product(a, b, da, db):
    return lax.dot_general(a, b, (((da,), (db,)), ((), ())), preferred_element_type=f32)


def sum_cores(weight, blocks, contract):
    send = product(weight, blocks[1], contract, 1).astype(bf16)
    got = to_group(send, 1)
    return product(weight, blocks[0], contract, 1) + got.astype(f32)


def finish(got, shift):
    total = jnp.sum(got.astype(f32), 0)
    turns = [total] + [
        jnp.concatenate([total[:, 384 - 96 * k :], total[:, : 384 - 96 * k]], 1) for k in (1, 2, 3)
    ]
    out = turns[3]
    for k in (0, 1, 2):
        out = jnp.where(shift == k, turns[k], out)
    return out.astype(bf16).T


def body(tokens, up_weight, down_weight, upstream):
    gy = lax.axis_index("gy")
    gz = lax.axis_index("gz")
    row = gy % 4
    high = gy >= 4
    chip, core = gz // 2, gz % 2

    up_own, up_far = spread_weight(up_weight, chip)
    ups = jnp.roll(upstream.reshape(4, 96, 768), -row, 0).reshape(384, 768)
    ups_core = to_group(ups, 1)
    ups_far = to_group(after(ups, up_own), 2)
    cut = cut_rows((ups, ups_core), down_weight, 1)
    first = send_rows(cut)
    toks = jnp.roll(tokens.reshape(4, 96, 768), -row, 0).reshape(384, 768)
    toks_core = to_group(toks, 1)
    toks_far = to_group(after(toks, up_own), 2)

    up_full = spread_cores(up_own, after(up_far, cut), chip, core)
    cut = cut_rows((toks, toks_core), up_full, 0)
    first = after(first, cut)
    second = send_rows(after(cut, *first))
    grad_mine, grad_theirs = send_half(first, high)

    ups_last = to_group(ups_far, 1)
    cut = cut_rows((ups_far, ups_last), down_weight, 1)
    second = after(second, cut)
    third = send_rows(after(cut, *second))
    pre_mine, pre_theirs = send_half(second, high)

    toks_last = to_group(toks_far, 1)
    cut = cut_rows((toks_far, toks_last), up_full, 0)
    third = after(third, cut)
    fourth = send_rows(after(cut, *third))
    value, slope = gelu_both(pre_mine + pre_theirs.astype(f32))
    pre_grad = (grad_mine + grad_theirs.astype(f32)) * slope
    near = pair_half(jnp.stack([pre_grad, value]).astype(bf16), high)
    grad_near_pair, act_near_pair = near[0], near[1]
    grad_mine, grad_theirs = send_half(third, high)
    fourth = after(fourth, near)

    fifth = gather_rows(after(grad_near_pair, *fourth))
    pre_mine, pre_theirs = send_half(fourth, high)
    value, slope = gelu_both(pre_mine + pre_theirs.astype(f32))
    act_far = value.astype(bf16)
    pre_grad = ((grad_mine + grad_theirs.astype(f32)) * slope).astype(bf16)
    grad_far_pair = pair_half(pre_grad, high)
    fifth = after(fifth, grad_far_pair)
    sixth = gather_rows(after(grad_far_pair, *fifth))
    act_far_pair = pair_half(act_far, high)
    grads_near = blocks_of(fifth)
    token_near = sum_cores(up_full, grads_near, 1)
    sixth = after(sixth, act_far_pair)

    seventh = gather_rows(after(act_far_pair, *sixth))
    grads_far = blocks_of(sixth)
    token_far_sum = sum_cores(up_full, grads_far, 1).astype(bf16)
    token_far = to_group(token_far_sum, 2)
    all_grads = jnp.concatenate(grads_near + grads_far, 0)
    all_tokens = jnp.concatenate([toks, toks_core, toks_far, toks_last], 0)
    up_grad = product(all_tokens, all_grads, 0, 0).astype(bf16)
    seventh = after(seventh, token_far_sum, up_grad)
    up_mine, up_theirs = collect_far(after(up_grad, token_far_sum), chip)

    eighth = gather_rows(after(act_near_pair, *seventh))
    token_total = (token_near + token_far.astype(f32)).astype(bf16).reshape(8, 96, 384)
    acts_far = blocks_of(after(seventh, token_total))
    out_far_sum = sum_cores(down_weight, acts_far, 0).astype(bf16)
    out_far = to_group(out_far_sum, 2)
    token_got = lax.all_to_all(after(token_total, out_far_sum), "gx", 0, 0, tiled=True)
    eighth = after(eighth, out_far_sum, up_theirs)

    acts_near = blocks_of(eighth)
    out_near = sum_cores(down_weight, acts_near, 0)
    out_total = (out_near + out_far.astype(f32)).astype(bf16).reshape(8, 96, 384)
    out_got = lax.all_to_all(after(out_total, token_got), "gx", 0, 0, tiled=True)

    up_out = collect_cores(up_mine, after(up_theirs, out_total), chip, core)
    token_grad = finish(after(token_got, out_total), row)
    mlp_output = finish(out_got, row)
    all_acts = jnp.concatenate(list(after(acts_near, out_total)) + acts_far, 0)
    all_ups = jnp.concatenate([ups, ups_core, ups_far, ups_last], 0)
    down_grad = product(all_acts, all_ups, 0, 0).astype(bf16)
    return (mlp_output, token_grad, up_out, down_grad)


def solution(mesh):
    return jax.shard_map(
        body,
        mesh=mesh,
        in_specs=(P("gz", "gy"), P(("gy", "gz"), "gx"), P(("gx", "gz"), "gy"), P("gz", "gy")),
        out_specs=(
            P("gz", ("gy", "gx")),
            P("gz", ("gy", "gx")),
            P(("gy", "gz"), "gx"),
            P(("gx", "gz"), "gy"),
        ),
        check_vma=False,
    )
```

```python
import jax
import jax.numpy as jnp
from jax import lax
from jax.sharding import PartitionSpec as P

coeff = 0.7978845608028654
cubic = 0.044715
f32 = jnp.float32
bf16 = jnp.bfloat16


def gelu_both(hidden):
    square = hidden * hidden
    inner = jnp.tanh(coeff * (hidden + cubic * hidden * square))
    value = 0.5 * hidden * (1.0 + inner)
    slope = 0.5 * (1.0 + inner) + 0.5 * hidden * (1.0 - inner * inner) * coeff * (
        1.0 + 3.0 * cubic * square
    )
    return value, slope


def to_group(x, flip):
    return lax.ppermute(x, "gz", [(i, i ^ flip) for i in range(4)])


def to_row(x, shift):
    return lax.ppermute(x, "gy", [(i, (i // 4) * 4 + (i + shift) % 4) for i in range(8)])


def to_half(x):
    return lax.ppermute(x, "gy", [(i, i ^ 4) for i in range(8)])


def after(x, *needed):
    return lax.optimization_barrier((x,) + needed)[0]


def spread_weight(shard, chip):
    send = lax.dynamic_slice_in_dim(shard, (1 - chip) * 1536, 1536, 1)
    return lax.dynamic_slice_in_dim(shard, chip * 1536, 1536, 1), to_group(send, 2)


def spread_cores(own, far, chip, core):
    both = jnp.stack([jnp.where(chip == 0, own, far), jnp.where(chip == 0, far, own)])
    mine = jnp.where(core == 0, both[:, :, :768], both[:, :, 768:])
    theirs = jnp.where(core == 0, both[:, :, 768:], both[:, :, :768])
    got = to_group(theirs, 1)
    return jnp.where(
        core == 0, jnp.stack([mine, got], 1), jnp.stack([got, mine], 1)
    ).reshape(768, 768)


def collect_far(full, chip):
    halves = full.reshape(2, 2, 192, 768)
    send = jnp.where(chip == 0, halves[1], halves[0])
    return jnp.where(chip == 0, halves[0], halves[1]), to_group(send, 2)


def collect_cores(own, far, chip, core):
    both = jnp.stack([jnp.where(chip == 0, own, far), jnp.where(chip == 0, far, own)])
    mine = jnp.where(core == 0, both[:, 0], both[:, 1])
    theirs = jnp.where(core == 0, both[:, 1], both[:, 0])
    got = to_group(theirs, 1)
    first = jnp.where(core == 0, mine, got)
    second = jnp.where(core == 0, got, mine)
    return jnp.concatenate([first[0], second[0], first[1], second[1]], 1)


def cut_rows(blocks, weight, contract):
    parts = [product(x, weight, 1, contract).astype(bf16) for x in blocks]
    return jnp.stack([p.reshape(4, 2, 48, 768) for p in parts], 1)


def send_rows(cut):
    return [cut[0]] + [to_row(cut[shift], shift) for shift in (1, 3, 2)]


def send_half(got, high):
    total = sum(g.astype(f32) for g in got)
    mine = jnp.where(high, total[:, 1], total[:, 0])
    theirs = jnp.where(high, total[:, 0], total[:, 1]).astype(bf16)
    return mine, to_half(theirs)


def pair_half(own, high):
    other = to_half(own)
    axis = own.ndim - 2
    return jnp.where(high, jnp.stack([other, own], axis), jnp.stack([own, other], axis))


def gather_rows(pair):
    return [pair, to_row(pair, 1), to_row(pair, 3), to_row(pair, 2)]


def blocks_of(got):
    pair, up, down, across = got
    return [
        jnp.concatenate([pair[r], down[r], across[r], up[r]], 0).reshape(384, 768)
        for r in range(2)
    ]


def product(a, b, da, db):
    return lax.dot_general(a, b, (((da,), (db,)), ((), ())), preferred_element_type=f32)


def sum_cores(weight, blocks, contract):
    send = product(weight, blocks[1], contract, 1).astype(bf16)
    got = to_group(send, 1)
    return product(weight, blocks[0], contract, 1) + got.astype(f32)


def turn_rows(x, shift):
    turns = [x] + [jnp.concatenate([x[96 * k :], x[: 96 * k]], 0) for k in (1, 2, 3)]
    out = turns[3]
    for k in (0, 1, 2):
        out = jnp.where(shift == k, turns[k], out)
    return out


def finish(got, shift):
    total = jnp.sum(got.astype(f32), 0)
    turns = [total] + [
        jnp.concatenate([total[:, 384 - 96 * k :], total[:, : 384 - 96 * k]], 1) for k in (1, 2, 3)
    ]
    out = turns[3]
    for k in (0, 1, 2):
        out = jnp.where(shift == k, turns[k], out)
    return out.astype(bf16).T


def body(tokens, up_weight, down_weight, upstream):
    gy = lax.axis_index("gy")
    gz = lax.axis_index("gz")
    row = gy % 4
    high = gy >= 4
    chip, core = gz // 2, gz % 2

    up_own, up_far = spread_weight(up_weight, chip)
    ups = turn_rows(upstream, row)
    ups_core = to_group(ups, 1)
    ups_far = to_group(after(ups, up_own), 2)
    cut = cut_rows((ups, ups_core), down_weight, 1)
    first = send_rows(cut)
    toks = turn_rows(tokens, row)
    toks_core = to_group(toks, 1)
    toks_far = to_group(after(toks, up_own), 2)

    up_full = spread_cores(up_own, after(up_far, cut), chip, core)
    cut = cut_rows((toks, toks_core), up_full, 0)
    first = after(first, cut)
    second = send_rows(after(cut, *first))
    grad_mine, grad_theirs = send_half(first, high)

    ups_last = to_group(ups_far, 1)
    cut = cut_rows((ups_far, ups_last), down_weight, 1)
    second = after(second, cut)
    third = send_rows(after(cut, *second))
    pre_mine, pre_theirs = send_half(second, high)

    toks_last = to_group(toks_far, 1)
    cut = cut_rows((toks_far, toks_last), up_full, 0)
    third = after(third, cut)
    fourth = send_rows(after(cut, *third))
    value, slope = gelu_both(pre_mine + pre_theirs.astype(f32))
    pre_grad = (grad_mine + grad_theirs.astype(f32)) * slope
    near = pair_half(jnp.stack([pre_grad, value]).astype(bf16), high)
    grad_near_pair, act_near_pair = near[0], near[1]
    grad_mine, grad_theirs = send_half(third, high)
    fourth = after(fourth, near)

    fifth = gather_rows(after(grad_near_pair, *fourth))
    pre_mine, pre_theirs = send_half(fourth, high)
    value, slope = gelu_both(pre_mine + pre_theirs.astype(f32))
    act_far = value.astype(bf16)
    pre_grad = ((grad_mine + grad_theirs.astype(f32)) * slope).astype(bf16)
    grad_far_pair = pair_half(pre_grad, high)
    fifth = after(fifth, grad_far_pair)
    sixth = gather_rows(after(grad_far_pair, *fifth))
    act_far_pair = pair_half(act_far, high)
    grads_near = blocks_of(fifth)
    token_near = sum_cores(up_full, grads_near, 1)
    sixth = after(sixth, act_far_pair)

    seventh = gather_rows(after(act_far_pair, *sixth))
    grads_far = blocks_of(sixth)
    token_far_sum = sum_cores(up_full, grads_far, 1).astype(bf16)
    token_far = to_group(token_far_sum, 2)
    all_grads = jnp.concatenate(grads_near + grads_far, 0)
    all_tokens = jnp.concatenate([toks, toks_core, toks_far, toks_last], 0)
    up_grad = product(all_tokens, all_grads, 0, 0).astype(bf16)
    seventh = after(seventh, token_far_sum, up_grad)
    up_mine, up_theirs = collect_far(after(up_grad, token_far_sum), chip)

    eighth = gather_rows(after(act_near_pair, *seventh))
    token_total = (token_near + token_far.astype(f32)).astype(bf16).reshape(8, 96, 384)
    acts_far = blocks_of(after(seventh, token_total))
    out_far_sum = sum_cores(down_weight, acts_far, 0).astype(bf16)
    out_far = to_group(out_far_sum, 2)
    token_got = lax.all_to_all(after(token_total, out_far_sum), "gx", 0, 0, tiled=True)
    eighth = after(eighth, out_far_sum, up_theirs)

    acts_near = blocks_of(eighth)
    out_near = sum_cores(down_weight, acts_near, 0)
    out_total = (out_near + out_far.astype(f32)).astype(bf16).reshape(8, 96, 384)
    out_got = lax.all_to_all(after(out_total, token_got), "gx", 0, 0, tiled=True)

    up_out = collect_cores(up_mine, after(up_theirs, out_total), chip, core)
    token_grad = finish(after(token_got, out_total), row)
    mlp_output = finish(out_got, row)
    all_acts = jnp.concatenate(list(after(acts_near, out_total)) + acts_far, 0)
    all_ups = jnp.concatenate([ups, ups_core, ups_far, ups_last], 0)
    down_grad = product(all_acts, all_ups, 0, 0).astype(bf16)
    return (mlp_output, token_grad, up_out, down_grad)


def solution(mesh):
    return jax.shard_map(
        body,
        mesh=mesh,
        in_specs=(P("gz", "gy"), P(("gy", "gz"), "gx"), P(("gx", "gz"), "gy"), P("gz", "gy")),
        out_specs=(
            P("gz", ("gy", "gx")),
            P("gz", ("gy", "gx")),
            P(("gy", "gz"), "gx"),
            P(("gx", "gz"), "gy"),
        ),
        check_vma=False,
    )
```
